32 devices in a mesh: dp: 8 (over y, x, core), hp: 4 (over z).
Axes of the slice: x: 2, y: 2, z: 4, core: 2. Of those that a mesh axis runs over, the one named last changes fastest.
Arguments:
- residual: bfloat16 [256, 7168], P('dp', 'hp'), may hold values from -60 to 60
- queries: bfloat16 [256, 128, 192], P('dp', 'hp'), may hold values from -48 to 48
- latent_cache: bfloat16 [256, 512, 576], P('dp'), may hold values from -4 to 4
- new_latent: bfloat16 [256, 576], P('dp'), may hold values from -4 to 4
- lengths: int32 [256], P('dp'), may hold values from 1 to 512, as said below
- w_absorb: bfloat16 [128, 128, 512], P('hp'), may hold values from -0.5 to 0.5
- w_value: bfloat16 [128, 512, 128], P('hp'), may hold values from -0.25 to 0.25
- w_out: bfloat16 [16384, 4, 1792], P('hp', None, 'dp'), may hold values from -0.046875 to 0.046875
- norm_gain: bfloat16 [7168], P('hp'), may hold values from 0.099609375 to 1.8984375
- w_gate: bfloat16 [7168, 18432], P('hp', 'dp'), may hold values from -0.0625 to 0.0625
- w_up: bfloat16 [7168, 18432], P('hp', 'dp'), may hold values from -0.0625 to 0.0625
- w_down: bfloat16 [18432, 7168], P('dp', 'hp'), may hold values from -0.046875 to 0.046875
Outputs:
- layer_out: bfloat16 [256, 7168], P('dp', 'hp')
The draws below stay inside these ranges and needn't reach their ends.
Inputs may be any that keep to these rules, and one draw needn't show every extreme that they name: `lengths`: some sample holds all 512 slots in every draw.
All inputs are finite; a program needn't handle non-finite values.
Results may differ from the reference program's by a relative error of at most 0.014.
Values may be sent and summed in bfloat16 or wider, within the bound.
A program may use at most 128 MiB of HBM per device.

```python
import math
import jax
import jax.numpy as jnp
from jax import lax

D = 7168
FF = 18432
HEADS = 128
NOPE = 128
ROPE = 64
LATENT = 512
VDIM = 128
CTX = 512
SAMPLES = 256
ROWPARTS = 4
DBLK = 1792


def attention_parts(key):
    folded = jax.random.fold_in(key, 7)
    subkeys = jax.random.split(folded, 3)
    entry_width = LATENT + ROPE
    cache_rows = jnp.clip(jax.random.normal(subkeys[0], (SAMPLES, CTX, entry_width), jnp.float32), -4.0, 4.0)
    query_rows = jnp.clip(jax.random.normal(subkeys[1], (SAMPLES, HEADS, NOPE + ROPE), jnp.float32), -4.0, 4.0)
    fresh_rows = jnp.clip(jax.random.normal(subkeys[2], (SAMPLES, entry_width), jnp.float32), -4.0, 4.0)
    return (cache_rows, query_rows, fresh_rows)


def draw_latent_cache(key, part):
    return attention_parts(key)[0].astype(jnp.bfloat16)


def draw_queries(key, part):
    return attention_parts(key)[1].astype(jnp.bfloat16)


def draw_new_latent(key, part):
    return attention_parts(key)[2].astype(jnp.bfloat16)


def draw_residual(key, part):
    subkeys = jax.random.split(jax.random.fold_in(key, 23), 2)
    column = jnp.arange(D, dtype=jnp.float32) / D
    spread = jax.random.uniform(subkeys[1], (D,), jnp.float32)
    values = jnp.clip(jax.random.normal(subkeys[0], (SAMPLES, D), jnp.float32), -4.0, 4.0)
    col_scale = 3.0 ** (column - 0.5) * 2.0 ** (spread - 0.5)
    return (values * col_scale[None, :]).astype(jnp.bfloat16)


def draw_lengths(key, part):
    subkeys = jax.random.split(jax.random.fold_in(key, 31), 2)
    drawn = jax.random.randint(subkeys[0], (SAMPLES,), 1, CTX + 1, jnp.int32)
    fullest = jax.random.randint(subkeys[1], (), 0, SAMPLES, jnp.int32)
    return jnp.where(jnp.arange(SAMPLES, dtype=jnp.int32) == fullest, CTX, drawn).astype(jnp.int32)


def block_scale(key, dims, cuts, smallest, top_value):
    level = 1.0
    for position, shards_of in cuts:
        steps = jax.random.uniform(jax.random.fold_in(jax.random.fold_in(key, 6), position), (shards_of,), jnp.float32, smallest / len(cuts), top_value / len(cuts))
        level = level * jnp.repeat(jnp.exp(steps), dims[position] // shards_of).reshape((-1,) + (1,) * (len(dims) - 1 - position))
    return level


def centred(stream_key, extent, width, reach, cuts=(), kind=jnp.bfloat16):
    result = width * jax.random.normal(stream_key, extent, jnp.float32)
    if cuts:
        result = result * block_scale(stream_key, extent, cuts, -0.22, 0.18)
    return jnp.clip(result, -reach, reach).astype(kind)


def setup_inputs(seed: int = 0) -> dict:
    seeds = jax.random.split(jax.random.key(seed), 13)
    return {
        "residual": draw_residual(jax.random.fold_in(seeds[12], 71), 0),
        "queries": draw_queries(jax.random.fold_in(seeds[12], 71), 0),
        "latent_cache": draw_latent_cache(jax.random.fold_in(seeds[12], 71), 0),
        "new_latent": draw_new_latent(jax.random.fold_in(seeds[12], 71), 0),
        "lengths": draw_lengths(jax.random.fold_in(seeds[12], 71), 0),
        "w_absorb": centred(seeds[5], (HEADS, NOPE, LATENT), NOPE ** -0.5, 0.5, ((0, 4),)),
        "w_value": centred(seeds[6], (HEADS, LATENT, VDIM), LATENT ** -0.5, 0.25, ((0, 4),)),
        "w_out": centred(seeds[7], (HEADS * VDIM, ROWPARTS, DBLK), (HEADS * VDIM) ** -0.5, 0.046875, ((0, 4), (2, 8))),
        "norm_gain": jnp.clip(1.0 + 0.18 * jax.random.normal(seeds[8], (D,), jnp.float32), 0.099609375, 1.8984375).astype(jnp.bfloat16),
        "w_gate": centred(seeds[9], (D, FF), D ** -0.5, 0.0625, ((0, 4), (1, 8))),
        "w_up": centred(seeds[10], (D, FF), D ** -0.5, 0.0625, ((0, 4), (1, 8))),
        "w_down": centred(seeds[11], (FF, D), FF ** -0.5, 0.046875, ((0, 8), (1, 4))),
    }


def sample_latent(operands):
    query_full, cache_rows, fresh_row, length = operands
    softmax_scale = 1.0 / math.sqrt(NOPE + ROPE)
    positions = jnp.arange(CTX, dtype=jnp.int32)
    query_wide = query_full.astype(jnp.float32)
    scores = jnp.einsum('hc,lc->hl', query_wide, cache_rows.astype(jnp.float32)) * softmax_scale
    scores = jnp.where(positions[None, :] < length, scores, -1e+30)
    own_score = jnp.einsum('hc,c->h', query_wide, fresh_row.astype(jnp.float32)) * softmax_scale
    peak = jnp.maximum(lax.optimization_barrier(jnp.max(scores, axis=1)), own_score)
    cached_exp = jnp.exp(scores - peak[:, None])
    own_exp = jnp.exp(own_score - peak)
    total = lax.optimization_barrier(jnp.sum(cached_exp, axis=1)) + own_exp
    probs_bf = (cached_exp / total[:, None]).astype(jnp.bfloat16)
    own_prob = (own_exp / total).astype(jnp.bfloat16)
    mixed = jnp.einsum('hl,lc->hc', probs_bf.astype(jnp.float32), cache_rows[:, :LATENT].astype(jnp.float32))
    mixed = mixed + own_prob.astype(jnp.float32)[:, None] * fresh_row[:LATENT].astype(jnp.float32)[None, :]
    return mixed.astype(jnp.bfloat16)

def reference(residual, queries, latent_cache, new_latent, lengths, w_absorb, w_value, w_out, norm_gain, w_gate, w_up, w_down):
    query_latent = jnp.einsum('shn,hnc->shc', queries[:, :, :NOPE].astype(jnp.float32), w_absorb.astype(jnp.float32)).astype(jnp.bfloat16)
    query_full = jnp.concatenate([query_latent, queries[:, :, NOPE:]], axis=2)
    head_latent = lax.map(sample_latent, (query_full, latent_cache, new_latent, lengths))
    head_values = jnp.einsum('shc,hcv->shv', head_latent.astype(jnp.float32), w_value.astype(jnp.float32)).astype(jnp.bfloat16)
    head_values = head_values.reshape(SAMPLES, HEADS * VDIM)
    attention_out = jnp.dot(head_values, w_out.reshape(HEADS * VDIM, D), preferred_element_type=jnp.float32).astype(jnp.bfloat16)
    hidden_state = residual.astype(jnp.float32) + attention_out.astype(jnp.float32)
    row_power = lax.optimization_barrier(jnp.sum(hidden_state * hidden_state, axis=1)) / D
    normed = (hidden_state * lax.rsqrt(row_power + 1e-06)[:, None] * norm_gain.astype(jnp.float32)[None, :]).astype(jnp.bfloat16)
    gate_sum = jnp.dot(normed, w_gate, preferred_element_type=jnp.float32)
    up_sum = jnp.dot(normed, w_up, preferred_element_type=jnp.float32)
    activated = (jax.nn.silu(gate_sum) * up_sum).astype(jnp.bfloat16)
    ffn_out = jnp.dot(activated, w_down, preferred_element_type=jnp.float32)
    return (hidden_state + ffn_out).astype(jnp.bfloat16)
```

```python
import functools
import math

import jax
import jax.numpy as jnp
from jax import lax
from jax.experimental import pallas as pl
from jax.experimental.pallas import tpu as pltpu
from jax.sharding import PartitionSpec as P

MESH = pl.DeviceIdType.MESH
LANES = 128
HOP = 2
GROUPS = 2


def ffn_kernel(
    hp_n, dp_n, model_width, h_ref, gain_ref, wg_hbm, wu_hbm, wd_hbm, out_ref,
    wgu, wd, u, part, act, stage, landed, power, scale,
    wgu_sem, wd_sem, part_send, part_recv, act_send, act_recv,
    down_send, down_recv, power_send, power_recv,
):
    me = lax.axis_index("hp")
    mine = lax.axis_index("dp")
    chunks, width = wgu.shape[0], wgu.shape[1]
    rows = out_ref.shape[0]
    sub = rows // GROUPS
    block = u.shape[1]
    last = hp_n - 1
    tile = 256 if width % 256 == 0 else LANES
    tiles = width // tile
    first_right = (chunks + 1) // 2
    flows = (
        (0, first_right, me, me + 1, me - 1),
        (first_right, chunks - first_right, last - me, me - 1, me + 1),
    )

    barrier = pltpu.get_barrier_semaphore()
    for j in range(1, hp_n):
        pl.semaphore_signal(
            barrier, inc=1, device_id=(mine, lax.rem(me + j, hp_n)), device_id_type=MESH
        )
    for j in range(1, dp_n):
        pl.semaphore_signal(
            barrier, inc=1, device_id=(lax.rem(mine + j, dp_n), me), device_id_type=MESH
        )

    def weight_copies(k):
        columns = pl.ds(k * LANES, LANES) if isinstance(k, int) else pl.ds(
            pl.multiple_of(k * LANES, LANES), LANES
        )
        return (
            pltpu.make_async_copy(
                wg_hbm.at[:, columns], wgu.at[k, :, pl.ds(0, LANES)], wgu_sem.at[k, 0]
            ),
            pltpu.make_async_copy(
                wu_hbm.at[:, columns], wgu.at[k, :, pl.ds(LANES, LANES)], wgu_sem.at[k, 1]
            ),
        )

    wd_copy = pltpu.make_async_copy(wd_hbm, wd, wd_sem)
    for step in range(first_right):
        for start, count, *_ in flows:
            if step < count:
                for copy in weight_copies(start + step):
                    copy.start()
    wd_copy.start()

    hidden = h_ref[...]
    scaled = (hidden * gain_ref[...].astype(jnp.float32)).astype(jnp.bfloat16)
    for g in range(GROUPS):
        for d in range(dp_n):
            u[g, d * sub : (d + 1) * sub, :] = scaled[
                d * rows + g * sub : d * rows + (g + 1) * sub
            ]
    squares = jnp.sum(hidden * hidden, axis=1, keepdims=True)
    squares = jnp.broadcast_to(squares, (squares.shape[0], LANES))
    power[me] = jnp.transpose(squares)[:8]

    pl.semaphore_wait(barrier, hp_n - 1 + dp_n - 1)

    def power_copy(source, target):
        return pltpu.make_async_remote_copy(
            src_ref=power.at[source],
            dst_ref=power.at[source],
            send_sem=power_send.at[target],
            recv_sem=power_recv.at[source],
            device_id=(mine, target),
            device_id_type=MESH,
        )

    for j in range(1, hp_n):
        power_copy(me, lax.rem(me + j, hp_n)).start()

    def finish_power():
        for j in range(1, hp_n):
            power_copy(lax.rem(me + j, hp_n), me).wait_recv()
        total = power[0, :1]
        for j in range(1, hp_n):
            total = total + power[j, :1]
        factor = lax.rsqrt(total / model_width + 1e-06)
        factor = jnp.transpose(jnp.broadcast_to(factor, (LANES, factor.shape[1])))
        for g in range(GROUPS):
            for d in range(dp_n):
                scale[g, d * sub : (d + 1) * sub, :] = factor[
                    d * rows + g * sub : d * rows + (g + 1) * sub
                ]

    def chunk_copy(buffer, send, recv, k, g, target):
        return pltpu.make_async_remote_copy(
            src_ref=buffer.at[k, g],
            dst_ref=buffer.at[k, g],
            send_sem=send.at[k, g],
            recv_sem=recv.at[k, g],
            device_id=(mine, target),
            device_id_type=MESH,
        )

    def add_partial(flow, t):
        start, count, place, after, before = flow
        c = t - HOP * place

        @pl.when(jnp.logical_and(c >= 0, c < count * GROUPS))
        def _():
            g = c // count
            k = start + c % count

            @pl.when(g == 0)
            def _():
                for copy in weight_copies(k):
                    copy.wait()

            own = jnp.dot(u[g], wgu[k], preferred_element_type=jnp.float32)

            @pl.when(place == 0)
            def _():
                part[k, g] = own.astype(jnp.bfloat16)

            @pl.when(place > 0)
            def _():
                chunk_copy(part, part_send, part_recv, k, g, me).wait_recv()

            @pl.when(jnp.logical_and(place > 0, place < last))
            def _():
                part[k, g] = (part[k, g].astype(jnp.float32) + own).astype(jnp.bfloat16)

            @pl.when(place < last)
            def _():
                chunk_copy(part, part_send, part_recv, k, g, after).start()

            @pl.when(place == last)
            def _():
                full = part[k, g].astype(jnp.float32) + own
                factor = scale[g]
                gate = full[:, :LANES] * factor
                up = full[:, LANES:] * factor
                act[k, g] = (gate / (1.0 + jnp.exp(-gate)) * up).astype(jnp.bfloat16)
                chunk_copy(act, act_send, act_recv, k, g, before).start()

    def pass_act(flow, t):
        start, count, place, after, before = flow
        c = t - HOP * (2 * last - place)

        @pl.when(jnp.logical_and(place < last, jnp.logical_and(c >= 0, c < count * GROUPS)))
        def _():
            g = c // count
            k = start + c % count
            chunk_copy(act, act_send, act_recv, k, g, me).wait_recv()

            @pl.when(place > 0)
            def _():
                chunk_copy(act, act_send, act_recv, k, g, before).start()

    def down_tile(g, n):
        columns = pl.ds(pl.multiple_of(n * tile, tile), tile)
        rows_in = jnp.concatenate([act[k, g] for k in range(chunks)], axis=1)
        result = jnp.dot(
            rows_in, wd[:, columns], preferred_element_type=jnp.float32
        ).astype(jnp.bfloat16)
        for d in range(dp_n):
            stage[g, d, :, columns] = result[d * sub : (d + 1) * sub]

    def down_copy(g, source, target):
        return pltpu.make_async_remote_copy(
            src_ref=stage.at[g, target],
            dst_ref=landed.at[g, source],
            send_sem=down_send.at[g, target],
            recv_sem=down_recv.at[g, source],
            device_id=(target, me),
            device_id_type=MESH,
        )

    def send_down(g):
        for j in range(1, dp_n):
            down_copy(g, mine, lax.rem(mine + j, dp_n)).start()
        landed[g, mine] = stage[g, mine]

    ready = first_right + 2 * HOP * last
    steps = max(first_right * GROUPS + 2 * HOP * last, ready + tiles)

    @pl.loop(0, steps)
    def _(t):
        @pl.when(t == HOP * last)
        def _():
            finish_power()

        for flow in flows:
            pass_act(flow, t)
        for flow in flows:
            add_partial(flow, t)

        @pl.when(t == ready)
        def _():
            wd_copy.wait()

        @pl.when(jnp.logical_and(t >= ready, t < ready + tiles))
        def _():
            down_tile(0, t - ready)

        @pl.when(t == ready + tiles - 1)
        def _():
            send_down(0)

    @pl.loop(0, tiles)
    def _(n):
        down_tile(1, n)

    send_down(1)

    result = h_ref[pl.ds(pl.multiple_of(mine * rows, rows), rows), :]
    for g in range(GROUPS):
        for j in range(1, dp_n):
            down_copy(g, lax.rem(mine + j, dp_n), mine).wait_recv()
    for g in range(GROUPS):
        total = result[g * sub : (g + 1) * sub]
        for d in range(dp_n):
            total = total + landed[g, d].astype(jnp.float32)
        out_ref[g * sub : (g + 1) * sub, :] = total.astype(jnp.bfloat16)

    for j in range(1, hp_n):
        power_copy(me, lax.rem(me + j, hp_n)).wait_send()
    for g in range(GROUPS):
        for j in range(1, dp_n):
            down_copy(g, mine, lax.rem(mine + j, dp_n)).wait_send()
    for start, count, place, after, before in flows:

        @pl.loop(start, start + count)
        def _(k):
            for g in range(GROUPS):

                @pl.when(place < last)
                def _():
                    chunk_copy(part, part_send, part_recv, k, g, me).wait_send()

                @pl.when(place > 0)
                def _():
                    chunk_copy(act, act_send, act_recv, k, g, me).wait_send()


def feed_forward(hidden_state, norm_gain, w_gate, w_up, w_down, rows):
    hp_n, dp_n = lax.axis_size("hp"), lax.axis_size("dp")
    samples, width = hidden_state.shape
    hidden_units = w_gate.shape[1]
    chunks = hidden_units // LANES
    block = samples // GROUPS
    sub = rows // GROUPS
    bf16, f32 = jnp.bfloat16, jnp.float32
    dma = pltpu.SemaphoreType.DMA
    any_space = pl.BlockSpec(memory_space=pl.ANY)
    vmem = pl.BlockSpec(memory_space=pltpu.VMEM)
    return pl.pallas_call(
        functools.partial(ffn_kernel, hp_n, dp_n, width * hp_n),
        out_shape=jax.ShapeDtypeStruct((rows, width), bf16),
        in_specs=[vmem, vmem, any_space, any_space, any_space],
        out_specs=vmem,
        scratch_shapes=[
            pltpu.VMEM((chunks, width, 2 * LANES), bf16),
            pltpu.VMEM((hidden_units, width), bf16),
            pltpu.VMEM((GROUPS, block, width), bf16),
            pltpu.VMEM((chunks, GROUPS, block, 2 * LANES), bf16),
            pltpu.VMEM((chunks, GROUPS, block, LANES), bf16),
            pltpu.VMEM((GROUPS, dp_n, sub, width), bf16),
            pltpu.VMEM((GROUPS, dp_n, sub, width), bf16),
            pltpu.VMEM((hp_n, 8, samples), f32),
            pltpu.VMEM((GROUPS, block, LANES), f32),
            dma((chunks, 2)),
            dma,
            dma((chunks, GROUPS)),
            dma((chunks, GROUPS)),
            dma((chunks, GROUPS)),
            dma((chunks, GROUPS)),
            dma((GROUPS, dp_n)),
            dma((GROUPS, dp_n)),
            dma((hp_n,)),
            dma((hp_n,)),
        ],
        compiler_params=pltpu.CompilerParams(
            collective_id=0, has_side_effects=True, vmem_limit_bytes=50 * 2**20
        ),
        cost_estimate=pl.CostEstimate(
            flops=6 * samples * width * hidden_units,
            bytes_accessed=6 * width * hidden_units,
            transcendentals=samples * hidden_units,
        ),
        name="feed_forward",
    )(hidden_state, norm_gain.reshape(1, -1), w_gate, w_up, w_down)


def on_device(
    residual,
    queries,
    latent_cache,
    new_latent,
    lengths,
    w_absorb,
    w_value,
    w_out,
    norm_gain,
    w_gate,
    w_up,
    w_down,
):
    sample_rows = queries.shape[0]
    nope_width = w_absorb.shape[1]
    latent_width = w_absorb.shape[2]
    softmax_scale = 1.0 / math.sqrt(queries.shape[2])
    all_residual = lax.all_gather(residual, "dp", axis=0, tiled=True)
    query_latent = jnp.einsum(
        "shn,hnc->shc", queries[:, :, :nope_width], w_absorb, preferred_element_type=jnp.float32
    ).astype(jnp.bfloat16)
    query_full = jnp.concatenate([query_latent, queries[:, :, nope_width:]], axis=2)
    scores = (
        jnp.einsum("shc,slc->shl", query_full, latent_cache, preferred_element_type=jnp.float32)
        * softmax_scale
    )
    positions = lax.broadcasted_iota(jnp.int32, (1, 1, latent_cache.shape[1]), 2)
    scores = jnp.where(positions < lengths[:, None, None], scores, -1e30)
    own_score = (
        jnp.einsum("shc,sc->sh", query_full, new_latent, preferred_element_type=jnp.float32)
        * softmax_scale
    )
    peak = jnp.maximum(jnp.max(scores, axis=2), own_score)
    cached_exp = jnp.exp(scores - peak[:, :, None])
    own_exp = jnp.exp(own_score - peak)
    total = jnp.sum(cached_exp, axis=2) + own_exp
    probs_bf = (cached_exp / total[:, :, None]).astype(jnp.bfloat16)
    own_prob = (own_exp / total).astype(jnp.bfloat16)
    head_latent = jnp.einsum(
        "shl,slc->shc",
        probs_bf,
        latent_cache[:, :, :latent_width],
        preferred_element_type=jnp.float32,
    )
    head_latent = head_latent + own_prob.astype(jnp.float32)[:, :, None] * new_latent[
        :, None, :latent_width
    ].astype(jnp.float32)
    head_latent = head_latent.astype(jnp.bfloat16)
    head_values = jnp.einsum(
        "shc,hcv->shv", head_latent, w_value, preferred_element_type=jnp.float32
    ).astype(jnp.bfloat16)
    head_values = head_values.reshape(sample_rows, -1)
    w_flat = w_out.reshape(w_out.shape[0], -1)
    partial_out = jnp.dot(
        lax.all_gather(head_values, "dp", axis=0, tiled=True),
        w_flat,
        preferred_element_type=jnp.float32,
    )
    partial_out = partial_out.reshape(partial_out.shape[0], w_out.shape[1], w_out.shape[2])
    summed_block = lax.psum_scatter(
        partial_out.astype(jnp.bfloat16), "hp", scatter_dimension=1, tiled=True
    )
    attention_out = lax.all_gather(summed_block, "dp", axis=2, tiled=True)
    attention_out = attention_out.reshape(attention_out.shape[0], -1)
    hidden_state = all_residual.astype(jnp.float32) + attention_out.astype(jnp.float32)
    return feed_forward(hidden_state, norm_gain, w_gate, w_up, w_down, sample_rows)


def solution(mesh):
    in_specs = (
        P("dp", "hp"),
        P("dp", "hp", None),
        P("dp", None, None),
        P("dp", None),
        P("dp"),
        P("hp", None, None),
        P("hp", None, None),
        P("hp", None, "dp"),
        P("hp"),
        P("hp", "dp"),
        P("hp", "dp"),
        P("dp", "hp"),
    )
    out_specs = P("dp", "hp")
    return jax.shard_map(
        on_device, mesh=mesh, in_specs=in_specs, out_specs=out_specs, check_vma=False
    )
```

```python
import functools
import math

import jax
import jax.numpy as jnp
from jax import lax
from jax.experimental import pallas as pl
from jax.experimental.pallas import tpu as pltpu
from jax.sharding import PartitionSpec as P

MESH = pl.DeviceIdType.MESH
LANES = 128
HOP = 2
GROUPS = 2


def flip(index, bits):
    for bit in bits:
        index = index + bit - 2 * bit * (index // bit % 2)
    return index


class Spread:
    def __init__(self, dp_n, mine, me, view, send, recv):
        bits = [1 << b for b in range(1, dp_n.bit_length() - 1)]
        self.orders = (bits + [1], bits[::-1] + [1])
        self.mine, self.me, self.view, self.send, self.recv = mine, me, view, send, recv
        self.plans = []
        for order in self.orders:
            offsets = [()]
            sends = []
            for phase, bit in enumerate(order):
                sends += [(phase, offset) for offset in offsets]
                offsets = offsets + [offset + (bit,) for offset in offsets]
            self.plans.append((offsets, sends))

    def copy(self, half, phase, offset):
        block = flip(self.mine, offset)
        place = self.plans[half][1].index((phase, offset))
        return pltpu.make_async_remote_copy(
            src_ref=self.view(block, half),
            dst_ref=self.view(block, half),
            send_sem=self.send.at[half, place],
            recv_sem=self.recv.at[half, block],
            device_id=(flip(self.mine, (self.orders[half][phase],)), self.me),
            device_id_type=MESH,
        )

    def arrived(self, half, offset):
        block = flip(self.mine, offset)
        pltpu.make_async_remote_copy(
            src_ref=self.view(block, half),
            dst_ref=self.view(block, half),
            send_sem=self.send.at[half, 0],
            recv_sem=self.recv.at[half, block],
            device_id=(flip(self.mine, (1,)), self.me),
            device_id_type=MESH,
        ).wait_recv()

    def start(self):
        for phase in range(len(self.orders[0])):
            for half in range(2):
                self.copy(half, phase, ()).start()

    def relay(self):
        for place in range(1, len(self.plans[0][0])):
            for half in range(2):
                offset = self.plans[half][0][place]
                self.arrived(half, offset)
                for phase, sent in self.plans[half][1]:
                    if sent == offset:
                        self.copy(half, phase, offset).start()

    def finish(self):
        for half in range(2):
            for phase, offset in self.plans[half][1]:
                self.copy(half, phase, offset).wait_send()


def ffn_kernel(
    hp_n, dp_n, model_width, hv_ref, res_ref, wo_hbm, gain_ref, wg_hbm, wu_hbm, wd_hbm, out_ref,
    hv, res, wo, out_stage, out_land, attn, h_ref, wgu, wd, u, part, act, stage, landed, power, scale,
    wgu_sem, wd_sem, part_send, part_recv, act_send, act_recv,
    down_send, down_recv, power_send, power_recv,
    wo_sem, hv_send, hv_recv, res_send, res_recv, attn_send, attn_recv, out_send, out_recv,
):
    me = lax.axis_index("hp")
    mine = lax.axis_index("dp")
    chunks, width = wgu.shape[0], wgu.shape[1]
    rows = out_ref.shape[0]
    sub = rows // GROUPS
    block = u.shape[1]
    last = hp_n - 1
    tile = 256 if width % 256 == 0 else LANES
    tiles = width // tile
    first_right = (chunks + 1) // 2
    flows = (
        (0, first_right, me, me + 1, me - 1),
        (first_right, chunks - first_right, last - me, me - 1, me + 1),
    )

    barrier = pltpu.get_barrier_semaphore()
    for j in range(1, hp_n):
        pl.semaphore_signal(
            barrier, inc=1, device_id=(mine, lax.rem(me + j, hp_n)), device_id_type=MESH
        )
    for j in range(1, dp_n):
        pl.semaphore_signal(
            barrier, inc=1, device_id=(lax.rem(mine + j, dp_n), me), device_id_type=MESH
        )

    def weight_copies(k):
        columns = pl.ds(k * LANES, LANES) if isinstance(k, int) else pl.ds(
            pl.multiple_of(k * LANES, LANES), LANES
        )
        return (
            pltpu.make_async_copy(
                wg_hbm.at[:, columns], wgu.at[k, :, pl.ds(0, LANES)], wgu_sem.at[k, 0]
            ),
            pltpu.make_async_copy(
                wu_hbm.at[:, columns], wgu.at[k, :, pl.ds(LANES, LANES)], wgu_sem.at[k, 1]
            ),
        )

    wo_copy = pltpu.make_async_copy(wo_hbm, wo, wo_sem)
    wo_copy.start()
    wd_copy = pltpu.make_async_copy(wd_hbm, wd, wd_sem)
    for step in range(first_right):
        for start, count, *_ in flows:
            if step < count:
                for copy in weight_copies(start + step):
                    copy.start()
    wd_copy.start()

    hv[mine] = hv_ref[...]
    res[mine] = res_ref[...]
    pl.semaphore_wait(barrier, hp_n - 1 + dp_n - 1)

    half_rows = rows // 2
    half_samples = out_stage.shape[2] // 2

    def row_half(buffer):
        return lambda block, half: buffer.at[block, pl.ds(half * half_rows, half_rows)]

    hv_spread = Spread(dp_n, mine, me, row_half(hv), hv_send, hv_recv)
    res_spread = Spread(dp_n, mine, me, row_half(res), res_send, res_recv)
    attn_spread = Spread(
        dp_n, mine, me,
        lambda block, half: attn.at[block, :, pl.ds(half * half_samples, half_samples)],
        attn_send, attn_recv,
    )

    def out_copy(source, target):
        return pltpu.make_async_remote_copy(
            src_ref=out_stage.at[target],
            dst_ref=out_land.at[source],
            send_sem=out_send.at[target],
            recv_sem=out_recv.at[source],
            device_id=(mine, target),
            device_id_type=MESH,
        )

    hv_spread.start()
    hv_spread.relay()
    res_spread.start()
    wo_copy.wait()
    for j in range(1, hp_n + 1):
        target = lax.rem(me + j, hp_n)
        out_stage[target] = lax.dot_general(
            wo[target],
            hv[...].reshape(dp_n * rows, hv.shape[2]),
            (((1,), (1,)), ((), ())),
            preferred_element_type=jnp.float32,
        ).astype(jnp.bfloat16)
        if j < hp_n:
            out_copy(me, target).start()
    res_spread.relay()
    own_sum = out_stage[me].astype(jnp.float32)
    for j in range(1, hp_n):
        source = lax.rem(me + j, hp_n)
        out_copy(source, me).wait_recv()
        own_sum = own_sum + out_land[source].astype(jnp.float32)
    attn[mine] = own_sum.astype(jnp.bfloat16)
    attn_spread.start()
    attn_spread.relay()
    attn_rows = attn[...].astype(jnp.float32).reshape(h_ref.shape[1], h_ref.shape[0])
    h_ref[...] = jnp.transpose(attn_rows) + res[...].astype(jnp.float32).reshape(h_ref.shape)

    hidden = h_ref[...]
    scaled = (hidden * gain_ref[...].astype(jnp.float32)).astype(jnp.bfloat16)
    for g in range(GROUPS):
        for d in range(dp_n):
            u[g, d * sub : (d + 1) * sub, :] = scaled[
                d * rows + g * sub : d * rows + (g + 1) * sub
            ]
    squares = jnp.sum(hidden * hidden, axis=1, keepdims=True)
    squares = jnp.broadcast_to(squares, (squares.shape[0], LANES))
    power[me] = jnp.transpose(squares)[:8]

    def power_copy(source, target):
        return pltpu.make_async_remote_copy(
            src_ref=power.at[source],
            dst_ref=power.at[source],
            send_sem=power_send.at[target],
            recv_sem=power_recv.at[source],
            device_id=(mine, target),
            device_id_type=MESH,
        )

    for j in range(1, hp_n):
        power_copy(me, lax.rem(me + j, hp_n)).start()

    def finish_power():
        for j in range(1, hp_n):
            power_copy(lax.rem(me + j, hp_n), me).wait_recv()
        total = power[0, :1]
        for j in range(1, hp_n):
            total = total + power[j, :1]
        factor = lax.rsqrt(total / model_width + 1e-06)
        factor = jnp.transpose(jnp.broadcast_to(factor, (LANES, factor.shape[1])))
        for g in range(GROUPS):
            for d in range(dp_n):
                scale[g, d * sub : (d + 1) * sub, :] = factor[
                    d * rows + g * sub : d * rows + (g + 1) * sub
                ]

    def chunk_copy(buffer, send, recv, k, g, target):
        return pltpu.make_async_remote_copy(
            src_ref=buffer.at[k, g],
            dst_ref=buffer.at[k, g],
            send_sem=send.at[k, g],
            recv_sem=recv.at[k, g],
            device_id=(mine, target),
            device_id_type=MESH,
        )

    def add_partial(flow, t):
        start, count, place, after, before = flow
        c = t - HOP * place

        @pl.when(jnp.logical_and(c >= 0, c < count * GROUPS))
        def _():
            g = c // count
            k = start + c % count

            @pl.when(g == 0)
            def _():
                for copy in weight_copies(k):
                    copy.wait()

            own = jnp.dot(u[g], wgu[k], preferred_element_type=jnp.float32)

            @pl.when(place == 0)
            def _():
                part[k, g] = own.astype(jnp.bfloat16)

            @pl.when(place > 0)
            def _():
                chunk_copy(part, part_send, part_recv, k, g, me).wait_recv()

            @pl.when(jnp.logical_and(place > 0, place < last))
            def _():
                part[k, g] = (part[k, g].astype(jnp.float32) + own).astype(jnp.bfloat16)

            @pl.when(place < last)
            def _():
                chunk_copy(part, part_send, part_recv, k, g, after).start()

            @pl.when(place == last)
            def _():
                full = part[k, g].astype(jnp.float32) + own
                factor = scale[g]
                gate = full[:, :LANES] * factor
                up = full[:, LANES:] * factor
                act[k, g] = (gate / (1.0 + jnp.exp(-gate)) * up).astype(jnp.bfloat16)
                chunk_copy(act, act_send, act_recv, k, g, before).start()

    def pass_act(flow, t):
        start, count, place, after, before = flow
        c = t - HOP * (2 * last - place)

        @pl.when(jnp.logical_and(place < last, jnp.logical_and(c >= 0, c < count * GROUPS)))
        def _():
            g = c // count
            k = start + c % count
            chunk_copy(act, act_send, act_recv, k, g, me).wait_recv()

            @pl.when(place > 0)
            def _():
                chunk_copy(act, act_send, act_recv, k, g, before).start()

    def down_tile(g, n):
        columns = pl.ds(pl.multiple_of(n * tile, tile), tile)
        rows_in = jnp.concatenate([act[k, g] for k in range(chunks)], axis=1)
        result = jnp.dot(
            rows_in, wd[:, columns], preferred_element_type=jnp.float32
        ).astype(jnp.bfloat16)
        for d in range(dp_n):
            stage[g, d, :, columns] = result[d * sub : (d + 1) * sub]

    def down_copy(g, source, target):
        return pltpu.make_async_remote_copy(
            src_ref=stage.at[g, target],
            dst_ref=landed.at[g, source],
            send_sem=down_send.at[g, target],
            recv_sem=down_recv.at[g, source],
            device_id=(target, me),
            device_id_type=MESH,
        )

    def send_down(g):
        for j in range(1, dp_n):
            down_copy(g, mine, lax.rem(mine + j, dp_n)).start()
        landed[g, mine] = stage[g, mine]

    ready = first_right + 2 * HOP * last
    steps = max(first_right * GROUPS + 2 * HOP * last, ready + tiles)

    @pl.loop(0, steps)
    def _(t):
        @pl.when(t == HOP * last)
        def _():
            finish_power()

        for flow in flows:
            pass_act(flow, t)
        for flow in flows:
            add_partial(flow, t)

        @pl.when(t == ready)
        def _():
            wd_copy.wait()

        @pl.when(jnp.logical_and(t >= ready, t < ready + tiles))
        def _():
            down_tile(0, t - ready)

        @pl.when(t == ready + tiles - 1)
        def _():
            send_down(0)

    @pl.loop(0, tiles)
    def _(n):
        down_tile(1, n)

    send_down(1)

    result = h_ref[pl.ds(pl.multiple_of(mine * rows, rows), rows), :]
    for g in range(GROUPS):
        for j in range(1, dp_n):
            down_copy(g, lax.rem(mine + j, dp_n), mine).wait_recv()
    for g in range(GROUPS):
        total = result[g * sub : (g + 1) * sub]
        for d in range(dp_n):
            total = total + landed[g, d].astype(jnp.float32)
        out_ref[g * sub : (g + 1) * sub, :] = total.astype(jnp.bfloat16)

    for j in range(1, hp_n):
        power_copy(me, lax.rem(me + j, hp_n)).wait_send()
        out_copy(me, lax.rem(me + j, hp_n)).wait_send()
    for spread in (hv_spread, res_spread, attn_spread):
        spread.finish()
    for g in range(GROUPS):
        for j in range(1, dp_n):
            down_copy(g, mine, lax.rem(mine + j, dp_n)).wait_send()
    for start, count, place, after, before in flows:

        @pl.loop(start, start + count)
        def _(k):
            for g in range(GROUPS):

                @pl.when(place < last)
                def _():
                    chunk_copy(part, part_send, part_recv, k, g, me).wait_send()

                @pl.when(place > 0)
                def _():
                    chunk_copy(act, act_send, act_recv, k, g, me).wait_send()


def feed_forward(head_values, residual, w_out, norm_gain, w_gate, w_up, w_down):
    hp_n, dp_n = lax.axis_size("hp"), lax.axis_size("dp")
    rows, width = residual.shape
    samples = rows * dp_n
    w_rows = jnp.transpose(w_out, (1, 2, 0))
    features = w_rows.shape[1]
    hidden_units = w_gate.shape[1]
    chunks = hidden_units // LANES
    block = samples // GROUPS
    sub = rows // GROUPS
    bf16, f32 = jnp.bfloat16, jnp.float32
    dma = pltpu.SemaphoreType.DMA
    any_space = pl.BlockSpec(memory_space=pl.ANY)
    vmem = pl.BlockSpec(memory_space=pltpu.VMEM)
    return pl.pallas_call(
        functools.partial(ffn_kernel, hp_n, dp_n, width * hp_n),
        out_shape=jax.ShapeDtypeStruct((rows, width), bf16),
        in_specs=[vmem, vmem, any_space, vmem, any_space, any_space, any_space],
        out_specs=vmem,
        scratch_shapes=[
            pltpu.VMEM((dp_n,) + head_values.shape, bf16),
            pltpu.VMEM((dp_n,) + residual.shape, bf16),
            pltpu.VMEM(w_rows.shape, bf16),
            pltpu.VMEM((hp_n, features, samples), bf16),
            pltpu.VMEM((hp_n, features, samples), bf16),
            pltpu.VMEM((dp_n, features, samples), bf16),
            pltpu.VMEM((samples, width), f32),
            pltpu.VMEM((chunks, width, 2 * LANES), bf16),
            pltpu.VMEM((hidden_units, width), bf16),
            pltpu.VMEM((GROUPS, block, width), bf16),
            pltpu.VMEM((chunks, GROUPS, block, 2 * LANES), bf16),
            pltpu.VMEM((chunks, GROUPS, block, LANES), bf16),
            pltpu.VMEM((GROUPS, dp_n, sub, width), bf16),
            pltpu.VMEM((GROUPS, dp_n, sub, width), bf16),
            pltpu.VMEM((hp_n, 8, samples), f32),
            pltpu.VMEM((GROUPS, block, LANES), f32),
            dma((chunks, 2)),
            dma,
            dma((chunks, GROUPS)),
            dma((chunks, GROUPS)),
            dma((chunks, GROUPS)),
            dma((chunks, GROUPS)),
            dma((GROUPS, dp_n)),
            dma((GROUPS, dp_n)),
            dma((hp_n,)),
            dma((hp_n,)),
            dma,
            dma((2, dp_n - 1)),
            dma((2, dp_n)),
            dma((2, dp_n - 1)),
            dma((2, dp_n)),
            dma((2, dp_n - 1)),
            dma((2, dp_n)),
            dma((hp_n,)),
            dma((hp_n,)),
        ],
        compiler_params=pltpu.CompilerParams(
            collective_id=0, has_side_effects=True, vmem_limit_bytes=60 * 2**20
        ),
        cost_estimate=pl.CostEstimate(
            flops=6 * samples * width * hidden_units,
            bytes_accessed=6 * width * hidden_units,
            transcendentals=samples * hidden_units,
        ),
        name="feed_forward",
    )(head_values, residual, w_rows, norm_gain.reshape(1, -1), w_gate, w_up, w_down)


def on_device(
    residual,
    queries,
    latent_cache,
    new_latent,
    lengths,
    w_absorb,
    w_value,
    w_out,
    norm_gain,
    w_gate,
    w_up,
    w_down,
):
    sample_rows = queries.shape[0]
    nope_width = w_absorb.shape[1]
    latent_width = w_absorb.shape[2]
    softmax_scale = 1.0 / math.sqrt(queries.shape[2])
    query_latent = jnp.einsum(
        "shn,hnc->shc", queries[:, :, :nope_width], w_absorb, preferred_element_type=jnp.float32
    ).astype(jnp.bfloat16)
    query_full = jnp.concatenate([query_latent, queries[:, :, nope_width:]], axis=2)
    scores = (
        jnp.einsum("shc,slc->shl", query_full, latent_cache, preferred_element_type=jnp.float32)
        * softmax_scale
    )
    positions = lax.broadcasted_iota(jnp.int32, (1, 1, latent_cache.shape[1]), 2)
    scores = jnp.where(positions < lengths[:, None, None], scores, -1e30)
    own_score = (
        jnp.einsum("shc,sc->sh", query_full, new_latent, preferred_element_type=jnp.float32)
        * softmax_scale
    )
    peak = jnp.maximum(jnp.max(scores, axis=2), own_score)
    cached_exp = jnp.exp(scores - peak[:, :, None])
    own_exp = jnp.exp(own_score - peak)
    total = jnp.sum(cached_exp, axis=2) + own_exp
    probs_bf = (cached_exp / total[:, :, None]).astype(jnp.bfloat16)
    own_prob = (own_exp / total).astype(jnp.bfloat16)
    head_latent = jnp.einsum(
        "shl,slc->shc",
        probs_bf,
        latent_cache[:, :, :latent_width],
        preferred_element_type=jnp.float32,
    )
    head_latent = head_latent + own_prob.astype(jnp.float32)[:, :, None] * new_latent[
        :, None, :latent_width
    ].astype(jnp.float32)
    head_latent = head_latent.astype(jnp.bfloat16)
    head_values = jnp.einsum(
        "shc,hcv->shv", head_latent, w_value, preferred_element_type=jnp.float32
    ).astype(jnp.bfloat16)
    head_values = head_values.reshape(sample_rows, -1)
    return feed_forward(head_values, residual, w_out, norm_gain, w_gate, w_up, w_down)


def solution(mesh):
    in_specs = (
        P("dp", "hp"),
        P("dp", "hp", None),
        P("dp", None, None),
        P("dp", None),
        P("dp"),
        P("hp", None, None),
        P("hp", None, None),
        P("hp", None, "dp"),
        P("hp"),
        P("hp", "dp"),
        P("hp", "dp"),
        P("dp", "hp"),
    )
    out_specs = P("dp", "hp")
    return jax.shard_map(
        on_device, mesh=mesh, in_specs=in_specs, out_specs=out_specs, check_vma=False
    )
```

```python
import functools
import math

import jax
import jax.numpy as jnp
from jax import lax
from jax.experimental import pallas as pl
from jax.experimental.pallas import tpu as pltpu
from jax.sharding import PartitionSpec as P

MESH = pl.DeviceIdType.MESH
LANES = 128
HOP = 2
GROUPS = 2


def flip(index, bits):
    for bit in bits:
        index = index + bit - 2 * bit * (index // bit % 2)
    return index


class Spread:
    def __init__(self, dp_n, mine, me, view, send, recv):
        bits = [1 << b for b in range(1, dp_n.bit_length() - 1)]
        self.orders = (bits + [1], bits[::-1] + [1])
        self.mine, self.me, self.view, self.send, self.recv = mine, me, view, send, recv
        self.plans = []
        for order in self.orders:
            offsets = [()]
            sends = []
            for phase, bit in enumerate(order):
                sends += [(phase, offset) for offset in offsets]
                offsets = offsets + [offset + (bit,) for offset in offsets]
            self.plans.append((offsets, sends))

    def copy(self, half, phase, offset):
        block = flip(self.mine, offset)
        place = self.plans[half][1].index((phase, offset))
        return pltpu.make_async_remote_copy(
            src_ref=self.view(block, half),
            dst_ref=self.view(block, half),
            send_sem=self.send.at[half, place],
            recv_sem=self.recv.at[half, block],
            device_id=(flip(self.mine, (self.orders[half][phase],)), self.me),
            device_id_type=MESH,
        )

    def arrived(self, half, offset):
        block = flip(self.mine, offset)
        pltpu.make_async_remote_copy(
            src_ref=self.view(block, half),
            dst_ref=self.view(block, half),
            send_sem=self.send.at[half, 0],
            recv_sem=self.recv.at[half, block],
            device_id=(flip(self.mine, (1,)), self.me),
            device_id_type=MESH,
        ).wait_recv()

    def start(self):
        for phase in range(len(self.orders[0])):
            for half in range(2):
                self.copy(half, phase, ()).start()

    def relay(self, first=1, stop=None):
        for place in range(len(self.plans[0][0]))[first:stop]:
            for half in range(2):
                offset = self.plans[half][0][place]
                self.arrived(half, offset)
                for phase, sent in self.plans[half][1]:
                    if sent == offset:
                        self.copy(half, phase, offset).start()

    def finish(self):
        for half in range(2):
            for phase, offset in self.plans[half][1]:
                self.copy(half, phase, offset).wait_send()


def layer_kernel(
    hp_n, dp_n, model_width, softmax_scale, len_ref, q_ref, kt_hbm, new_ref, wv_hbm, res_ref, wo_hbm, gain_ref, wg_hbm, wu_hbm, wd_hbm, out_ref,
    kbuf, latent, wv, hv, res, wo, out_stage, out_land, attn, h_ref, wgu, wd, u, part, act, stage, landed, power, scale,
    wgu_sem, wd_sem, part_send, part_recv, act_send, act_recv,
    down_send, down_recv, power_send, power_recv,
    wo_sem, hv_send, hv_recv, res_send, res_recv, attn_send, attn_recv, out_send, out_recv,
    kbuf_sem, wv_sem, hv_send2, hv_recv2,
):
    me = lax.axis_index("hp")
    mine = lax.axis_index("dp")
    chunks, width = wgu.shape[0], wgu.shape[1]
    rows = out_ref.shape[0]
    sub = rows // GROUPS
    block = u.shape[1]
    last = hp_n - 1
    tile = 256 if width % 256 == 0 else LANES
    tiles = width // tile
    first_right = (chunks + 1) // 2
    flows = (
        (0, first_right, me, me + 1, me - 1),
        (first_right, chunks - first_right, last - me, me - 1, me + 1),
    )

    barrier = pltpu.get_barrier_semaphore()
    for j in range(1, hp_n):
        pl.semaphore_signal(
            barrier, inc=1, device_id=(mine, lax.rem(me + j, hp_n)), device_id_type=MESH
        )
    for j in range(1, dp_n):
        pl.semaphore_signal(
            barrier, inc=1, device_id=(lax.rem(mine + j, dp_n), me), device_id_type=MESH
        )

    def weight_copies(k):
        columns = pl.ds(k * LANES, LANES) if isinstance(k, int) else pl.ds(
            pl.multiple_of(k * LANES, LANES), LANES
        )
        return (
            pltpu.make_async_copy(
                wg_hbm.at[:, columns], wgu.at[k, :, pl.ds(0, LANES)], wgu_sem.at[k, 0]
            ),
            pltpu.make_async_copy(
                wu_hbm.at[:, columns], wgu.at[k, :, pl.ds(LANES, LANES)], wgu_sem.at[k, 1]
            ),
        )

    wo_copy = pltpu.make_async_copy(wo_hbm, wo, wo_sem)
    wd_copy = pltpu.make_async_copy(wd_hbm, wd, wd_sem)
    wv_copy = pltpu.make_async_copy(wv_hbm, wv, wv_sem)

    def start_weights():
        wo_copy.start()
        for step in range(first_right):
            for start, count, *_ in flows:
                if step < count:
                    for copy in weight_copies(start + step):
                        copy.start()
        wd_copy.start()

    def cache_copy(sample):
        slot = lax.rem(sample, kbuf.shape[0])
        return pltpu.make_async_copy(kt_hbm.at[sample], kbuf.at[slot], kbuf_sem.at[slot])

    ahead = kbuf.shape[0] - 1
    for sample in range(ahead):
        cache_copy(sample).start()
    wv_copy.start()

    res[mine] = res_ref[...]
    pl.semaphore_wait(barrier, hp_n - 1 + dp_n - 1)

    half_rows = rows // 2
    half_samples = out_stage.shape[2] // 2

    def row_half(buffer):
        return lambda block, half: buffer.at[block, pl.ds(half * half_rows, half_rows)]

    half_values = hv.shape[2] // 2

    def value_part(part_rows):
        return lambda block, half: hv.at[
            block, pl.ds(part_rows * half_rows, half_rows), pl.ds(half * half_values, half_values)
        ]

    hv_spreads = (
        Spread(dp_n, mine, me, value_part(0), hv_send, hv_recv),
        Spread(dp_n, mine, me, value_part(1), hv_send2, hv_recv2),
    )
    res_spread = Spread(dp_n, mine, me, row_half(res), res_send, res_recv)
    attn_spread = Spread(
        dp_n, mine, me,
        lambda block, half: attn.at[block, :, pl.ds(half * half_samples, half_samples)],
        attn_send, attn_recv,
    )

    def out_copy(source, target):
        return pltpu.make_async_remote_copy(
            src_ref=out_stage.at[target],
            dst_ref=out_land.at[source],
            send_sem=out_send.at[target],
            recv_sem=out_recv.at[source],
            device_id=(mine, target),
            device_id_type=MESH,
        )

    latent_width = latent.shape[2]
    value_width = wv.shape[2]
    positions = lax.broadcasted_iota(jnp.int32, (q_ref.shape[1], kbuf.shape[2]), 1)

    def project(part_rows):
        @pl.loop(0, wv.shape[0])
        def _(h):
            values = jnp.dot(
                latent[h].astype(jnp.bfloat16), wv[h], preferred_element_type=jnp.float32
            )
            hv[
                mine,
                part_rows * half_rows : (part_rows + 1) * half_rows,
                pl.ds(pl.multiple_of(h * value_width, value_width), value_width),
            ] = values.astype(jnp.bfloat16)

    res_spread.start()

    @pl.loop(0, rows)
    def _(sample):
        @pl.when(sample + ahead < rows)
        def _():
            cache_copy(sample + ahead).start()

        cache_copy(sample).wait()
        slot = lax.rem(sample, kbuf.shape[0])
        query = q_ref[sample]
        fresh = new_ref[sample]
        scores = jnp.dot(query, kbuf[slot], preferred_element_type=jnp.float32) * softmax_scale
        scores = jnp.where(positions < len_ref[sample], scores, -1e30)
        own_score = (
            jnp.sum(query.astype(jnp.float32) * fresh, axis=1, keepdims=True) * softmax_scale
        )
        peak = jnp.maximum(jnp.max(scores, axis=1, keepdims=True), own_score)
        cached_exp = jnp.exp(scores - peak)
        own_exp = jnp.exp(own_score - peak)
        total = jnp.sum(cached_exp, axis=1, keepdims=True) + own_exp
        probs = (cached_exp / total).astype(jnp.bfloat16)
        own_prob = (own_exp / total).astype(jnp.bfloat16).astype(jnp.float32)
        mixed = lax.dot_general(
            probs,
            kbuf[slot, :latent_width],
            (((1,), (1,)), ((), ())),
            preferred_element_type=jnp.float32,
        )
        mixed = mixed + own_prob * fresh[:, :latent_width]
        latent[:, pl.ds(lax.rem(sample, half_rows), 1), :] = mixed.reshape(
            mixed.shape[0], 1, latent_width
        )

        @pl.when(sample == half_rows - 1)
        def _():
            wv_copy.wait()
            project(0)
            hv_spreads[0].start()
            start_weights()
            res_spread.relay()

        @pl.when(sample == rows * 5 // 8)
        def _():
            hv_spreads[0].relay(1, 2)

        @pl.when(sample == rows * 3 // 4)
        def _():
            hv_spreads[0].relay(2, 4)

        @pl.when(sample == rows * 7 // 8)
        def _():
            hv_spreads[0].relay(4, 6)

    project(1)
    hv_spreads[1].start()
    hv_spreads[0].relay(6)
    hv_spreads[1].relay()
    wo_copy.wait()
    for j in range(1, hp_n + 1):
        target = lax.rem(me + j, hp_n)
        out_stage[target] = lax.dot_general(
            wo[target],
            hv[...].reshape(dp_n * rows, hv.shape[2]),
            (((1,), (1,)), ((), ())),
            preferred_element_type=jnp.float32,
        ).astype(jnp.bfloat16)
        if j < hp_n:
            out_copy(me, target).start()
    own_sum = out_stage[me].astype(jnp.float32)
    for j in range(1, hp_n):
        source = lax.rem(me + j, hp_n)
        out_copy(source, me).wait_recv()
        own_sum = own_sum + out_land[source].astype(jnp.float32)
    attn[mine] = own_sum.astype(jnp.bfloat16)
    attn_spread.start()
    attn_spread.relay()
    attn_rows = attn[...].astype(jnp.float32).reshape(h_ref.shape[1], h_ref.shape[0])
    h_ref[...] = jnp.transpose(attn_rows) + res[...].astype(jnp.float32).reshape(h_ref.shape)

    hidden = h_ref[...]
    scaled = (hidden * gain_ref[...].astype(jnp.float32)).astype(jnp.bfloat16)
    for g in range(GROUPS):
        for d in range(dp_n):
            u[g, d * sub : (d + 1) * sub, :] = scaled[
                d * rows + g * sub : d * rows + (g + 1) * sub
            ]
    squares = jnp.sum(hidden * hidden, axis=1, keepdims=True)
    squares = jnp.broadcast_to(squares, (squares.shape[0], LANES))
    power[me] = jnp.transpose(squares)[:8]

    def power_copy(source, target):
        return pltpu.make_async_remote_copy(
            src_ref=power.at[source],
            dst_ref=power.at[source],
            send_sem=power_send.at[target],
            recv_sem=power_recv.at[source],
            device_id=(mine, target),
            device_id_type=MESH,
        )

    for j in range(1, hp_n):
        power_copy(me, lax.rem(me + j, hp_n)).start()

    def finish_power():
        for j in range(1, hp_n):
            power_copy(lax.rem(me + j, hp_n), me).wait_recv()
        total = power[0, :1]
        for j in range(1, hp_n):
            total = total + power[j, :1]
        factor = lax.rsqrt(total / model_width + 1e-06)
        factor = jnp.transpose(jnp.broadcast_to(factor, (LANES, factor.shape[1])))
        for g in range(GROUPS):
            for d in range(dp_n):
                scale[g, d * sub : (d + 1) * sub, :] = factor[
                    d * rows + g * sub : d * rows + (g + 1) * sub
                ]

    def chunk_copy(buffer, send, recv, k, g, target):
        return pltpu.make_async_remote_copy(
            src_ref=buffer.at[k, g],
            dst_ref=buffer.at[k, g],
            send_sem=send.at[k, g],
            recv_sem=recv.at[k, g],
            device_id=(mine, target),
            device_id_type=MESH,
        )

    def add_partial(flow, t):
        start, count, place, after, before = flow
        c = t - HOP * place

        @pl.when(jnp.logical_and(c >= 0, c < count * GROUPS))
        def _():
            g = c // count
            k = start + c % count

            @pl.when(g == 0)
            def _():
                for copy in weight_copies(k):
                    copy.wait()

            own = jnp.dot(u[g], wgu[k], preferred_element_type=jnp.float32)

            @pl.when(place == 0)
            def _():
                part[k, g] = own.astype(jnp.bfloat16)

            @pl.when(place > 0)
            def _():
                chunk_copy(part, part_send, part_recv, k, g, me).wait_recv()

            @pl.when(jnp.logical_and(place > 0, place < last))
            def _():
                part[k, g] = (part[k, g].astype(jnp.float32) + own).astype(jnp.bfloat16)

            @pl.when(place < last)
            def _():
                chunk_copy(part, part_send, part_recv, k, g, after).start()

            @pl.when(place == last)
            def _():
                full = part[k, g].astype(jnp.float32) + own
                factor = scale[g]
                gate = full[:, :LANES] * factor
                up = full[:, LANES:] * factor
                act[k, g] = (gate / (1.0 + jnp.exp(-gate)) * up).astype(jnp.bfloat16)
                chunk_copy(act, act_send, act_recv, k, g, before).start()

    def pass_act(flow, t):
        start, count, place, after, before = flow
        c = t - HOP * (2 * last - place)

        @pl.when(jnp.logical_and(place < last, jnp.logical_and(c >= 0, c < count * GROUPS)))
        def _():
            g = c // count
            k = start + c % count
            chunk_copy(act, act_send, act_recv, k, g, me).wait_recv()

            @pl.when(place > 0)
            def _():
                chunk_copy(act, act_send, act_recv, k, g, before).start()

    def down_tile(g, n):
        columns = pl.ds(pl.multiple_of(n * tile, tile), tile)
        rows_in = jnp.concatenate([act[k, g] for k in range(chunks)], axis=1)
        result = jnp.dot(
            rows_in, wd[:, columns], preferred_element_type=jnp.float32
        ).astype(jnp.bfloat16)
        for d in range(dp_n):
            stage[g, d, :, columns] = result[d * sub : (d + 1) * sub]

    def down_copy(g, source, target):
        return pltpu.make_async_remote_copy(
            src_ref=stage.at[g, target],
            dst_ref=landed.at[g, source],
            send_sem=down_send.at[g, target],
            recv_sem=down_recv.at[g, source],
            device_id=(target, me),
            device_id_type=MESH,
        )

    def send_down(g):
        for j in range(1, dp_n):
            down_copy(g, mine, lax.rem(mine + j, dp_n)).start()
        landed[g, mine] = stage[g, mine]

    ready = first_right + 2 * HOP * last
    steps = max(first_right * GROUPS + 2 * HOP * last, ready + tiles)

    @pl.loop(0, steps)
    def _(t):
        @pl.when(t == HOP * last)
        def _():
            finish_power()

        for flow in flows:
            pass_act(flow, t)
        for flow in flows:
            add_partial(flow, t)

        @pl.when(t == ready)
        def _():
            wd_copy.wait()

        @pl.when(jnp.logical_and(t >= ready, t < ready + tiles))
        def _():
            down_tile(0, t - ready)

        @pl.when(t == ready + tiles - 1)
        def _():
            send_down(0)

    @pl.loop(0, tiles)
    def _(n):
        down_tile(1, n)

    send_down(1)

    result = h_ref[pl.ds(pl.multiple_of(mine * rows, rows), rows), :]
    for g in range(GROUPS):
        for j in range(1, dp_n):
            down_copy(g, lax.rem(mine + j, dp_n), mine).wait_recv()
    for g in range(GROUPS):
        total = result[g * sub : (g + 1) * sub]
        for d in range(dp_n):
            total = total + landed[g, d].astype(jnp.float32)
        out_ref[g * sub : (g + 1) * sub, :] = total.astype(jnp.bfloat16)

    for j in range(1, hp_n):
        power_copy(me, lax.rem(me + j, hp_n)).wait_send()
        out_copy(me, lax.rem(me + j, hp_n)).wait_send()
    for spread in hv_spreads + (res_spread, attn_spread):
        spread.finish()
    for g in range(GROUPS):
        for j in range(1, dp_n):
            down_copy(g, mine, lax.rem(mine + j, dp_n)).wait_send()
    for start, count, place, after, before in flows:

        @pl.loop(start, start + count)
        def _(k):
            for g in range(GROUPS):

                @pl.when(place < last)
                def _():
                    chunk_copy(part, part_send, part_recv, k, g, me).wait_send()

                @pl.when(place > 0)
                def _():
                    chunk_copy(act, act_send, act_recv, k, g, me).wait_send()


def layer(softmax_scale, lengths, query_full, latent_cache, new_latent, w_value, residual, w_out, norm_gain, w_gate, w_up, w_down):
    hp_n, dp_n = lax.axis_size("hp"), lax.axis_size("dp")
    rows, width = residual.shape
    samples = rows * dp_n
    heads, latent_width, value_width = w_value.shape
    cache_rows = jnp.transpose(latent_cache, (0, 2, 1))
    new_rows = new_latent.astype(jnp.float32)[:, None, :]
    w_rows = jnp.transpose(w_out, (1, 2, 0))
    features = w_rows.shape[1]
    hidden_units = w_gate.shape[1]
    chunks = hidden_units // LANES
    block = samples // GROUPS
    sub = rows // GROUPS
    bf16, f32 = jnp.bfloat16, jnp.float32
    dma = pltpu.SemaphoreType.DMA
    any_space = pl.BlockSpec(memory_space=pl.ANY)
    vmem = pl.BlockSpec(memory_space=pltpu.VMEM)
    return pl.pallas_call(
        functools.partial(layer_kernel, hp_n, dp_n, width * hp_n, softmax_scale),
        out_shape=jax.ShapeDtypeStruct((rows, width), bf16),
        in_specs=[
            pl.BlockSpec(memory_space=pltpu.SMEM), vmem, any_space, vmem, any_space,
            vmem, any_space, vmem, any_space, any_space, any_space],
        out_specs=vmem,
        scratch_shapes=[
            pltpu.VMEM((4,) + cache_rows.shape[1:], bf16),
            pltpu.VMEM((heads, rows // 2, latent_width), f32),
            pltpu.VMEM(w_value.shape, bf16),
            pltpu.VMEM((dp_n, rows, heads * value_width), bf16),
            pltpu.VMEM((dp_n,) + residual.shape, bf16),
            pltpu.VMEM(w_rows.shape, bf16),
            pltpu.VMEM((hp_n, features, samples), bf16),
            pltpu.VMEM((hp_n, features, samples), bf16),
            pltpu.VMEM((dp_n, features, samples), bf16),
            pltpu.VMEM((samples, width), f32),
            pltpu.VMEM((chunks, width, 2 * LANES), bf16),
            pltpu.VMEM((hidden_units, width), bf16),
            pltpu.VMEM((GROUPS, block, width), bf16),
            pltpu.VMEM((chunks, GROUPS, block, 2 * LANES), bf16),
            pltpu.VMEM((chunks, GROUPS, block, LANES), bf16),
            pltpu.VMEM((GROUPS, dp_n, sub, width), bf16),
            pltpu.VMEM((GROUPS, dp_n, sub, width), bf16),
            pltpu.VMEM((hp_n, 8, samples), f32),
            pltpu.VMEM((GROUPS, block, LANES), f32),
            dma((chunks, 2)),
            dma,
            dma((chunks, GROUPS)),
            dma((chunks, GROUPS)),
            dma((chunks, GROUPS)),
            dma((chunks, GROUPS)),
            dma((GROUPS, dp_n)),
            dma((GROUPS, dp_n)),
            dma((hp_n,)),
            dma((hp_n,)),
            dma,
            dma((2, dp_n - 1)),
            dma((2, dp_n)),
            dma((2, dp_n - 1)),
            dma((2, dp_n)),
            dma((2, dp_n - 1)),
            dma((2, dp_n)),
            dma((hp_n,)),
            dma((hp_n,)),
            dma((4,)),
            dma,
            dma((2, dp_n - 1)),
            dma((2, dp_n)),
        ],
        compiler_params=pltpu.CompilerParams(
            collective_id=0, has_side_effects=True, vmem_limit_bytes=60 * 2**20
        ),
        cost_estimate=pl.CostEstimate(
            flops=6 * samples * width * hidden_units,
            bytes_accessed=6 * width * hidden_units,
            transcendentals=samples * hidden_units,
        ),
        name="layer",
    )(lengths, query_full, cache_rows, new_rows, w_value, residual, w_rows, norm_gain.reshape(1, -1), w_gate, w_up, w_down)


def on_device(
    residual,
    queries,
    latent_cache,
    new_latent,
    lengths,
    w_absorb,
    w_value,
    w_out,
    norm_gain,
    w_gate,
    w_up,
    w_down,
):
    sample_rows = queries.shape[0]
    nope_width = w_absorb.shape[1]
    softmax_scale = 1.0 / math.sqrt(queries.shape[2])
    query_latent = jnp.einsum(
        "shn,hnc->shc", queries[:, :, :nope_width], w_absorb, preferred_element_type=jnp.float32
    ).astype(jnp.bfloat16)
    query_full = jnp.concatenate([query_latent, queries[:, :, nope_width:]], axis=2)
    return layer(
        softmax_scale, lengths, query_full, latent_cache, new_latent, w_value, residual,
        w_out, norm_gain, w_gate, w_up, w_down,
    )


def solution(mesh):
    in_specs = (
        P("dp", "hp"),
        P("dp", "hp", None),
        P("dp", None, None),
        P("dp", None),
        P("dp"),
        P("hp", None, None),
        P("hp", None, None),
        P("hp", None, "dp"),
        P("hp"),
        P("hp", "dp"),
        P("hp", "dp"),
        P("dp", "hp"),
    )
    out_specs = P("dp", "hp")
    return jax.shard_map(
        on_device, mesh=mesh, in_specs=in_specs, out_specs=out_specs, check_vma=False
    )
```

```python
import functools
import math

import jax
import jax.numpy as jnp
from jax import lax
from jax.experimental import pallas as pl
from jax.experimental.pallas import tpu as pltpu
from jax.sharding import PartitionSpec as P

MESH = pl.DeviceIdType.MESH
LANES = 128
HOP = 2
GROUPS = 2
BATCH = 4
HEAD_BATCH = 8


def flip(index, bits):
    for bit in bits:
        index = index + bit - 2 * bit * (index // bit % 2)
    return index


class Spread:
    def __init__(self, dp_n, mine, me, view, send, recv):
        bits = [1 << b for b in range(1, dp_n.bit_length() - 1)]
        self.orders = (bits + [1], bits[::-1] + [1])
        self.mine, self.me, self.view, self.send, self.recv = mine, me, view, send, recv
        self.plans = []
        for order in self.orders:
            offsets = [()]
            sends = []
            for phase, bit in enumerate(order):
                sends += [(phase, offset) for offset in offsets]
                offsets = offsets + [offset + (bit,) for offset in offsets]
            self.plans.append((offsets, sends))

    def copy(self, half, phase, offset):
        block = flip(self.mine, offset)
        place = self.plans[half][1].index((phase, offset))
        return pltpu.make_async_remote_copy(
            src_ref=self.view(block, half),
            dst_ref=self.view(block, half),
            send_sem=self.send.at[half, place],
            recv_sem=self.recv.at[half, block],
            device_id=(flip(self.mine, (self.orders[half][phase],)), self.me),
            device_id_type=MESH,
        )

    def arrived(self, half, offset):
        block = flip(self.mine, offset)
        pltpu.make_async_remote_copy(
            src_ref=self.view(block, half),
            dst_ref=self.view(block, half),
            send_sem=self.send.at[half, 0],
            recv_sem=self.recv.at[half, block],
            device_id=(flip(self.mine, (1,)), self.me),
            device_id_type=MESH,
        ).wait_recv()

    def start(self):
        for phase in range(len(self.orders[0])):
            for half in range(2):
                self.copy(half, phase, ()).start()

    def relay(self, first=1, stop=None):
        for place in range(len(self.plans[0][0]))[first:stop]:
            for half in range(2):
                offset = self.plans[half][0][place]
                self.arrived(half, offset)
                for phase, sent in self.plans[half][1]:
                    if sent == offset:
                        self.copy(half, phase, offset).start()

    def finish(self):
        for half in range(2):
            for phase, offset in self.plans[half][1]:
                self.copy(half, phase, offset).wait_send()


def layer_kernel(
    hp_n, dp_n, model_width, softmax_scale, len_ref, q_ref, kt_hbm, new_ref, wv_hbm, res_ref, wo_hbm, gain_ref, wg_hbm, wu_hbm, wd_hbm, out_ref,
    kbuf, latent, wv, hv, res, wo, out_stage, out_land, attn, h_ref, wgu, wd, u, part, act, stage, landed, power, scale,
    wgu_sem, wd_sem, part_send, part_recv, act_send, act_recv,
    down_send, down_recv, power_send, power_recv,
    wo_sem, hv_send, hv_recv, res_send, res_recv, attn_send, attn_recv, out_send, out_recv,
    kbuf_sem, wv_sem, hv_send2, hv_recv2,
):
    me = lax.axis_index("hp")
    mine = lax.axis_index("dp")
    chunks, width = wgu.shape[0], wgu.shape[1]
    rows = out_ref.shape[0]
    sub = rows // GROUPS
    block = u.shape[1]
    last = hp_n - 1
    tile = 256 if width % 256 == 0 else LANES
    tiles = width // tile
    first_right = (chunks + 1) // 2
    flows = (
        (0, first_right, me, me + 1, me - 1),
        (first_right, chunks - first_right, last - me, me - 1, me + 1),
    )

    barrier = pltpu.get_barrier_semaphore()
    for j in range(1, hp_n):
        pl.semaphore_signal(
            barrier, inc=1, device_id=(mine, lax.rem(me + j, hp_n)), device_id_type=MESH
        )
    for j in range(1, dp_n):
        pl.semaphore_signal(
            barrier, inc=1, device_id=(lax.rem(mine + j, dp_n), me), device_id_type=MESH
        )

    def weight_copies(k):
        columns = pl.ds(k * LANES, LANES) if isinstance(k, int) else pl.ds(
            pl.multiple_of(k * LANES, LANES), LANES
        )
        return (
            pltpu.make_async_copy(
                wg_hbm.at[:, columns], wgu.at[k, :, pl.ds(0, LANES)], wgu_sem.at[k, 0]
            ),
            pltpu.make_async_copy(
                wu_hbm.at[:, columns], wgu.at[k, :, pl.ds(LANES, LANES)], wgu_sem.at[k, 1]
            ),
        )

    wo_copy = pltpu.make_async_copy(wo_hbm, wo, wo_sem)
    wd_copy = pltpu.make_async_copy(wd_hbm, wd, wd_sem)
    wv_copy = pltpu.make_async_copy(wv_hbm, wv, wv_sem)

    def start_weights():
        for step in range(first_right):
            for start, count, *_ in flows:
                if step < count:
                    for copy in weight_copies(start + step):
                        copy.start()
        wd_copy.start()

    def cache_copy(sample):
        slot = lax.rem(sample, kbuf.shape[0])
        return pltpu.make_async_copy(kt_hbm.at[sample], kbuf.at[slot], kbuf_sem.at[slot])

    for sample in range(BATCH):
        cache_copy(sample).start()
    wv_copy.start()

    res[mine] = res_ref[...]
    pl.semaphore_wait(barrier, hp_n - 1 + dp_n - 1)

    half_rows = rows // 2
    half_samples = out_stage.shape[2] // 2

    def row_half(buffer):
        return lambda block, half: buffer.at[block, pl.ds(half * half_rows, half_rows)]

    half_values = hv.shape[2] // 2

    def value_part(part_rows):
        return lambda block, half: hv.at[
            block, pl.ds(part_rows * half_rows, half_rows), pl.ds(half * half_values, half_values)
        ]

    hv_spreads = (
        Spread(dp_n, mine, me, value_part(0), hv_send, hv_recv),
        Spread(dp_n, mine, me, value_part(1), hv_send2, hv_recv2),
    )
    res_spread = Spread(dp_n, mine, me, row_half(res), res_send, res_recv)
    attn_spread = Spread(
        dp_n, mine, me,
        lambda block, half: attn.at[block, :, pl.ds(half * half_samples, half_samples)],
        attn_send, attn_recv,
    )

    def out_copy(source, target):
        return pltpu.make_async_remote_copy(
            src_ref=out_stage.at[target],
            dst_ref=out_land.at[source],
            send_sem=out_send.at[target],
            recv_sem=out_recv.at[source],
            device_id=(mine, target),
            device_id_type=MESH,
        )

    latent_width = latent.shape[2]
    value_width = wv.shape[2]
    positions = lax.broadcasted_iota(jnp.int32, (q_ref.shape[1], kbuf.shape[2]), 1)

    def project(part_rows):
        @pl.loop(0, wv.shape[0] // HEAD_BATCH)
        def _(turn):
            heads = [turn * HEAD_BATCH + b for b in range(HEAD_BATCH)]
            values = [
                jnp.dot(latent[h].astype(jnp.bfloat16), wv[h], preferred_element_type=jnp.float32)
                for h in heads
            ]
            width_all = value_width * HEAD_BATCH
            hv[
                mine,
                part_rows * half_rows : (part_rows + 1) * half_rows,
                pl.ds(pl.multiple_of(turn * width_all, width_all), width_all),
            ] = jnp.concatenate(values, axis=1).astype(jnp.bfloat16)

    res_spread.start()

    @pl.loop(0, rows // BATCH)
    def _(turn):
        @pl.when(turn + 1 < rows // BATCH)
        def _():
            for b in range(BATCH):
                cache_copy((turn + 1) * BATCH + b).start()

        samples = [turn * BATCH + b for b in range(BATCH)]
        slots = [lax.rem(turn, 2) * BATCH + b for b in range(BATCH)]
        for sample in samples:
            cache_copy(sample).wait()
        scores = []
        own_scores = []
        for sample, slot in zip(samples, slots):
            query = q_ref[sample]
            score = jnp.dot(query, kbuf[slot], preferred_element_type=jnp.float32)
            scores.append(
                jnp.where(positions < len_ref[sample], score * softmax_scale, -1e30)
            )
            own_scores.append(
                jnp.sum(query.astype(jnp.float32) * new_ref[sample], axis=1, keepdims=True)
                * softmax_scale
            )
        scores = jnp.concatenate(scores, axis=0)
        own_score = jnp.concatenate(own_scores, axis=0)
        peak = jnp.maximum(jnp.max(scores, axis=1, keepdims=True), own_score)
        cached_exp = jnp.exp(scores - peak)
        own_exp = jnp.exp(own_score - peak)
        total = jnp.sum(cached_exp, axis=1, keepdims=True) + own_exp
        probs = (cached_exp * (1.0 / total)).astype(jnp.bfloat16)
        own_prob = (own_exp / total).astype(jnp.bfloat16).astype(jnp.float32)
        heads = q_ref.shape[1]
        for b, (sample, slot) in enumerate(zip(samples, slots)):
            mixed = lax.dot_general(
                probs[b * heads : (b + 1) * heads],
                kbuf[slot, :latent_width],
                (((1,), (1,)), ((), ())),
                preferred_element_type=jnp.float32,
            )
            mixed = mixed + own_prob[b * heads : (b + 1) * heads] * new_ref[sample][:, :latent_width]
            latent[:, pl.ds(lax.rem(sample, half_rows), 1), :] = mixed.reshape(
                heads, 1, latent_width
            )

        @pl.when(turn == half_rows // BATCH - 1)
        def _():
            wv_copy.wait()
            project(0)
            hv_spreads[0].start()
            wo_copy.start()
            res_spread.relay()

        @pl.when(turn == rows * 5 // 8 // BATCH)
        def _():
            hv_spreads[0].relay(1, 2)

        @pl.when(turn == rows * 3 // 4 // BATCH)
        def _():
            hv_spreads[0].relay(2, 4)

        @pl.when(turn == rows * 7 // 8 // BATCH)
        def _():
            hv_spreads[0].relay(4, 6)

    start_weights()
    project(1)
    hv_spreads[1].start()
    hv_spreads[0].relay(6)
    hv_spreads[1].relay()
    wo_copy.wait()
    for j in range(1, hp_n + 1):
        target = lax.rem(me + j, hp_n)
        out_stage[target] = lax.dot_general(
            wo[target],
            hv[...].reshape(dp_n * rows, hv.shape[2]),
            (((1,), (1,)), ((), ())),
            preferred_element_type=jnp.float32,
        ).astype(jnp.bfloat16)
        if j < hp_n:
            out_copy(me, target).start()
    own_sum = out_stage[me].astype(jnp.float32)
    for j in range(1, hp_n):
        source = lax.rem(me + j, hp_n)
        out_copy(source, me).wait_recv()
        own_sum = own_sum + out_land[source].astype(jnp.float32)
    attn[mine] = own_sum.astype(jnp.bfloat16)
    attn_spread.start()
    attn_spread.relay()
    attn_rows = attn[...].astype(jnp.float32).reshape(h_ref.shape[1], h_ref.shape[0])
    h_ref[...] = jnp.transpose(attn_rows) + res[...].astype(jnp.float32).reshape(h_ref.shape)

    hidden = h_ref[...]
    scaled = (hidden * gain_ref[...].astype(jnp.float32)).astype(jnp.bfloat16)
    for g in range(GROUPS):
        for d in range(dp_n):
            u[g, d * sub : (d + 1) * sub, :] = scaled[
                d * rows + g * sub : d * rows + (g + 1) * sub
            ]
    squares = jnp.sum(hidden * hidden, axis=1, keepdims=True)
    squares = jnp.broadcast_to(squares, (squares.shape[0], LANES))
    power[me] = jnp.transpose(squares)[:8]

    def power_copy(source, target):
        return pltpu.make_async_remote_copy(
            src_ref=power.at[source],
            dst_ref=power.at[source],
            send_sem=power_send.at[target],
            recv_sem=power_recv.at[source],
            device_id=(mine, target),
            device_id_type=MESH,
        )

    for j in range(1, hp_n):
        power_copy(me, lax.rem(me + j, hp_n)).start()

    def finish_power():
        for j in range(1, hp_n):
            power_copy(lax.rem(me + j, hp_n), me).wait_recv()
        total = power[0, :1]
        for j in range(1, hp_n):
            total = total + power[j, :1]
        factor = lax.rsqrt(total / model_width + 1e-06)
        factor = jnp.transpose(jnp.broadcast_to(factor, (LANES, factor.shape[1])))
        for g in range(GROUPS):
            for d in range(dp_n):
                scale[g, d * sub : (d + 1) * sub, :] = factor[
                    d * rows + g * sub : d * rows + (g + 1) * sub
                ]

    def chunk_copy(buffer, send, recv, k, g, target):
        return pltpu.make_async_remote_copy(
            src_ref=buffer.at[k, g],
            dst_ref=buffer.at[k, g],
            send_sem=send.at[k, g],
            recv_sem=recv.at[k, g],
            device_id=(mine, target),
            device_id_type=MESH,
        )

    def add_partial(flow, t):
        start, count, place, after, before = flow
        c = t - HOP * place

        @pl.when(jnp.logical_and(c >= 0, c < count * GROUPS))
        def _():
            g = c // count
            k = start + c % count

            @pl.when(g == 0)
            def _():
                for copy in weight_copies(k):
                    copy.wait()

            own = jnp.dot(u[g], wgu[k], preferred_element_type=jnp.float32)

            @pl.when(place == 0)
            def _():
                part[k, g] = own.astype(jnp.bfloat16)

            @pl.when(place > 0)
            def _():
                chunk_copy(part, part_send, part_recv, k, g, me).wait_recv()

            @pl.when(jnp.logical_and(place > 0, place < last))
            def _():
                part[k, g] = (part[k, g].astype(jnp.float32) + own).astype(jnp.bfloat16)

            @pl.when(place < last)
            def _():
                chunk_copy(part, part_send, part_recv, k, g, after).start()

            @pl.when(place == last)
            def _():
                full = part[k, g].astype(jnp.float32) + own
                factor = scale[g]
                gate = full[:, :LANES] * factor
                up = full[:, LANES:] * factor
                act[k, g] = (gate / (1.0 + jnp.exp(-gate)) * up).astype(jnp.bfloat16)
                chunk_copy(act, act_send, act_recv, k, g, before).start()

    def pass_act(flow, t):
        start, count, place, after, before = flow
        c = t - HOP * (2 * last - place)

        @pl.when(jnp.logical_and(place < last, jnp.logical_and(c >= 0, c < count * GROUPS)))
        def _():
            g = c // count
            k = start + c % count
            chunk_copy(act, act_send, act_recv, k, g, me).wait_recv()

            @pl.when(place > 0)
            def _():
                chunk_copy(act, act_send, act_recv, k, g, before).start()

    def down_tile(g, n):
        columns = pl.ds(pl.multiple_of(n * tile, tile), tile)
        rows_in = jnp.concatenate([act[k, g] for k in range(chunks)], axis=1)
        result = jnp.dot(
            rows_in, wd[:, columns], preferred_element_type=jnp.float32
        ).astype(jnp.bfloat16)
        for d in range(dp_n):
            stage[g, d, :, columns] = result[d * sub : (d + 1) * sub]

    def down_copy(g, source, target):
        return pltpu.make_async_remote_copy(
            src_ref=stage.at[g, target],
            dst_ref=landed.at[g, source],
            send_sem=down_send.at[g, target],
            recv_sem=down_recv.at[g, source],
            device_id=(target, me),
            device_id_type=MESH,
        )

    def send_down(g):
        for j in range(1, dp_n):
            down_copy(g, mine, lax.rem(mine + j, dp_n)).start()
        landed[g, mine] = stage[g, mine]

    ready = first_right + 2 * HOP * last
    steps = max(first_right * GROUPS + 2 * HOP * last, ready + tiles)

    @pl.loop(0, steps)
    def _(t):
        @pl.when(t == HOP * last)
        def _():
            finish_power()

        for flow in flows:
            pass_act(flow, t)
        for flow in flows:
            add_partial(flow, t)

        @pl.when(t == ready)
        def _():
            wd_copy.wait()

        @pl.when(jnp.logical_and(t >= ready, t < ready + tiles))
        def _():
            down_tile(0, t - ready)

        @pl.when(t == ready + tiles - 1)
        def _():
            send_down(0)

    @pl.loop(0, tiles)
    def _(n):
        down_tile(1, n)

    send_down(1)

    result = h_ref[pl.ds(pl.multiple_of(mine * rows, rows), rows), :]
    for g in range(GROUPS):
        for j in range(1, dp_n):
            down_copy(g, lax.rem(mine + j, dp_n), mine).wait_recv()
    for g in range(GROUPS):
        total = result[g * sub : (g + 1) * sub]
        for d in range(dp_n):
            total = total + landed[g, d].astype(jnp.float32)
        out_ref[g * sub : (g + 1) * sub, :] = total.astype(jnp.bfloat16)

    for j in range(1, hp_n):
        power_copy(me, lax.rem(me + j, hp_n)).wait_send()
        out_copy(me, lax.rem(me + j, hp_n)).wait_send()
    for spread in hv_spreads + (res_spread, attn_spread):
        spread.finish()
    for g in range(GROUPS):
        for j in range(1, dp_n):
            down_copy(g, mine, lax.rem(mine + j, dp_n)).wait_send()
    for start, count, place, after, before in flows:

        @pl.loop(start, start + count)
        def _(k):
            for g in range(GROUPS):

                @pl.when(place < last)
                def _():
                    chunk_copy(part, part_send, part_recv, k, g, me).wait_send()

                @pl.when(place > 0)
                def _():
                    chunk_copy(act, act_send, act_recv, k, g, me).wait_send()


def layer(softmax_scale, lengths, query_full, latent_cache, new_latent, w_value, residual, w_out, norm_gain, w_gate, w_up, w_down):
    hp_n, dp_n = lax.axis_size("hp"), lax.axis_size("dp")
    rows, width = residual.shape
    samples = rows * dp_n
    heads, latent_width, value_width = w_value.shape
    cache_rows = jnp.transpose(latent_cache, (0, 2, 1))
    new_rows = new_latent.astype(jnp.float32)[:, None, :]
    w_rows = jnp.transpose(w_out, (1, 2, 0))
    features = w_rows.shape[1]
    hidden_units = w_gate.shape[1]
    chunks = hidden_units // LANES
    block = samples // GROUPS
    sub = rows // GROUPS
    bf16, f32 = jnp.bfloat16, jnp.float32
    dma = pltpu.SemaphoreType.DMA
    any_space = pl.BlockSpec(memory_space=pl.ANY)
    vmem = pl.BlockSpec(memory_space=pltpu.VMEM)
    return pl.pallas_call(
        functools.partial(layer_kernel, hp_n, dp_n, width * hp_n, softmax_scale),
        out_shape=jax.ShapeDtypeStruct((rows, width), bf16),
        in_specs=[
            pl.BlockSpec(memory_space=pltpu.SMEM), vmem, any_space, vmem, any_space,
            vmem, any_space, vmem, any_space, any_space, any_space],
        out_specs=vmem,
        scratch_shapes=[
            pltpu.VMEM((2 * BATCH,) + cache_rows.shape[1:], bf16),
            pltpu.VMEM((heads, rows // 2, latent_width), f32),
            pltpu.VMEM(w_value.shape, bf16),
            pltpu.VMEM((dp_n, rows, heads * value_width), bf16),
            pltpu.VMEM((dp_n,) + residual.shape, bf16),
            pltpu.VMEM(w_rows.shape, bf16),
            pltpu.VMEM((hp_n, features, samples), bf16),
            pltpu.VMEM((hp_n, features, samples), bf16),
            pltpu.VMEM((dp_n, features, samples), bf16),
            pltpu.VMEM((samples, width), f32),
            pltpu.VMEM((chunks, width, 2 * LANES), bf16),
            pltpu.VMEM((hidden_units, width), bf16),
            pltpu.VMEM((GROUPS, block, width), bf16),
            pltpu.VMEM((chunks, GROUPS, block, 2 * LANES), bf16),
            pltpu.VMEM((chunks, GROUPS, block, LANES), bf16),
            pltpu.VMEM((GROUPS, dp_n, sub, width), bf16),
            pltpu.VMEM((GROUPS, dp_n, sub, width), bf16),
            pltpu.VMEM((hp_n, 8, samples), f32),
            pltpu.VMEM((GROUPS, block, LANES), f32),
            dma((chunks, 2)),
            dma,
            dma((chunks, GROUPS)),
            dma((chunks, GROUPS)),
            dma((chunks, GROUPS)),
            dma((chunks, GROUPS)),
            dma((GROUPS, dp_n)),
            dma((GROUPS, dp_n)),
            dma((hp_n,)),
            dma((hp_n,)),
            dma,
            dma((2, dp_n - 1)),
            dma((2, dp_n)),
            dma((2, dp_n - 1)),
            dma((2, dp_n)),
            dma((2, dp_n - 1)),
            dma((2, dp_n)),
            dma((hp_n,)),
            dma((hp_n,)),
            dma((2 * BATCH,)),
            dma,
            dma((2, dp_n - 1)),
            dma((2, dp_n)),
        ],
        compiler_params=pltpu.CompilerParams(
            collective_id=0, has_side_effects=True, vmem_limit_bytes=60 * 2**20
        ),
        cost_estimate=pl.CostEstimate(
            flops=6 * samples * width * hidden_units,
            bytes_accessed=6 * width * hidden_units,
            transcendentals=samples * hidden_units,
        ),
        name="layer",
    )(lengths, query_full, cache_rows, new_rows, w_value, residual, w_rows, norm_gain.reshape(1, -1), w_gate, w_up, w_down)


def on_device(
    residual,
    queries,
    latent_cache,
    new_latent,
    lengths,
    w_absorb,
    w_value,
    w_out,
    norm_gain,
    w_gate,
    w_up,
    w_down,
):
    sample_rows = queries.shape[0]
    nope_width = w_absorb.shape[1]
    softmax_scale = 1.0 / math.sqrt(queries.shape[2])
    query_latent = jnp.einsum(
        "shn,hnc->shc", queries[:, :, :nope_width], w_absorb, preferred_element_type=jnp.float32
    ).astype(jnp.bfloat16)
    query_full = jnp.concatenate([query_latent, queries[:, :, nope_width:]], axis=2)
    return layer(
        softmax_scale, lengths, query_full, latent_cache, new_latent, w_value, residual,
        w_out, norm_gain, w_gate, w_up, w_down,
    )


def solution(mesh):
    in_specs = (
        P("dp", "hp"),
        P("dp", "hp", None),
        P("dp", None, None),
        P("dp", None),
        P("dp"),
        P("hp", None, None),
        P("hp", None, None),
        P("hp", None, "dp"),
        P("hp"),
        P("hp", "dp"),
        P("hp", "dp"),
        P("dp", "hp"),
    )
    out_specs = P("dp", "hp")
    return jax.shard_map(
        on_device, mesh=mesh, in_specs=in_specs, out_specs=out_specs, check_vma=False
    )
```
